32 devices in a mesh: dom: 2 (over y), expert: 8 (over z, x), tensor: 2 (over core).
Axes of the slice: x: 2, y: 2, z: 4, core: 2. Of those that a mesh axis runs over, the one named last changes fastest.
Arguments:
- act: bfloat16 [2048, 2048], P(('dom', 'expert'), 'tensor'), parts along dimension 0, may hold values from -6 to 6
- grad_out: bfloat16 [2048, 2048], P(('dom', 'expert'), 'tensor'), parts along dimension 0, may hold values from -6 to 6
- route_ids: int32 [2048, 2], P(('dom', 'expert')), parts along dimension 0, may hold values from 0 to 15, as said below
- gate_probs: bfloat16 [2048, 2], P(('dom', 'expert')), parts along dimension 0, may hold values from 0.099609375 to 1
- w_gate: bfloat16 [2048, 57344], P(None, ('expert', 'tensor')), may hold values from -0.125 to 0.125
- w_up: bfloat16 [2048, 57344], P(None, ('expert', 'tensor')), may hold values from -0.125 to 0.125
- w_down: bfloat16 [57344, 2048], P(('expert', 'tensor')), may hold values from -0.046875 to 0.046875
Outputs:
- d_act: bfloat16 [2048, 2048], P(('dom', 'expert'), 'tensor'), parts along dimension 0
- d_gate: float32 [2048, 2], P(('dom', 'expert')), parts along dimension 0
- dw_gate: bfloat16 [4096, 57344], P('dom', ('expert', 'tensor')), parts along dimension 0
- dw_up: bfloat16 [4096, 57344], P('dom', ('expert', 'tensor')), parts along dimension 0
- dw_down: bfloat16 [57344, 4096], P(('expert', 'tensor'), 'dom'), parts along dimension 1
The draws below stay inside these ranges and needn't reach their ends.
There are 2 independent parts, one for each index of `dom`. The reference program is written for one: setup_inputs(seed, part) draws one part's arguments, and reference() takes and returns one part's arrays. A program takes and returns all parts, laid end to end along the dimension named above; an argument that names none is the same for every part. Nothing has to cross between parts.
Inputs may be any that keep to these rules, and one draw needn't show every extreme that they name: `route_ids`: the two ids of a token differ. Among the 128 tokens of one index of expert, each id below 4 is named by at most 8 tokens, and one id below 4, the same for all indices, is named by exactly 8 tokens of every index.
All inputs are finite; a program needn't handle non-finite values.
Results may differ from the reference program's by a relative error of at most 0.0051.
Values may be sent and summed in bfloat16 or wider, within the bound.
A program may use at most 192 MiB of HBM per device.

```python
import math
import jax
import jax.numpy as jnp

D = 2048
FFW = 14336
NEXP = 16
FLIGHT = 4
TOK_DEV = 128
CAP = 8
TOKENS = 1024
FW = 57344


def draw_route_ids(key, part):
    key = jax.random.fold_in(key, 17)
    streams = jax.random.split(key, 6)
    blocks = TOKENS // TOK_DEV
    full_one = jax.random.randint(streams[0], (), 0, FLIGHT)
    counts = jax.random.randint(streams[1], (blocks, FLIGHT), CAP // 3, CAP + 1)
    counts = jnp.where(jnp.arange(FLIGHT)[None, :] == full_one, CAP, counts)
    starts = jnp.cumsum(counts, axis=1) - counts
    filled = jnp.sum(counts, axis=1)
    position = jnp.arange(2 * TOK_DEV)
    owners = jnp.sum((position[None, :, None] >= starts[:, None, :]).astype(jnp.int32), axis=2) - 1
    in_window = position[None, :] < filled[:, None]
    first_other = jax.random.randint(streams[2], (blocks, TOK_DEV), FLIGHT, NEXP)
    offset = jax.random.randint(streams[3], (blocks, TOK_DEV), 1, NEXP - FLIGHT)
    second_other = FLIGHT + (first_other - FLIGHT + offset) % (NEXP - FLIGHT)
    others = jnp.concatenate([first_other, second_other], axis=1)
    by_rank = jnp.where(in_window, owners, others).reshape(blocks, 2, TOK_DEV)
    scores = jax.random.randint(streams[4], (blocks, TOK_DEV), 0, 1 << 20) * TOK_DEV + jnp.arange(TOK_DEV)[None, :]
    token_rank = jnp.argsort(jnp.argsort(scores, axis=1), axis=1)
    chosen = jnp.take_along_axis(by_rank, token_rank[:, None, :], axis=2)
    chosen = jnp.transpose(chosen, (0, 2, 1))
    swapped = jax.random.randint(streams[5], (blocks, TOK_DEV, 1), 0, 2)
    chosen = jnp.where(swapped == 1, chosen[:, :, ::-1], chosen)
    return chosen.reshape(TOKENS, 2).astype(jnp.int32)


def shard_levels(rng, shape, cuts, smallest, largest):
    factor_of = 1.0
    for dim, shards_of in cuts:
        draws = jax.random.uniform(jax.random.fold_in(jax.random.fold_in(rng, 6), dim), (shards_of,), jnp.float32, smallest / len(cuts), largest / len(cuts))
        factor_of = factor_of * jnp.repeat(jnp.exp(draws), shape[dim] // shards_of).reshape((-1,) + (1,) * (len(shape) - 1 - dim))
    return factor_of


def noise(stream_key, dims, width, limit, cuts=(), held_as=jnp.bfloat16):
    entries = width * jax.random.normal(stream_key, dims, jnp.float32)
    if cuts:
        entries = entries * shard_levels(stream_key, dims, cuts, -0.22, 0.18)
    return jnp.clip(entries, -limit, limit).astype(held_as)


def setup_inputs(seed: int = 0, part: int = 0) -> dict:
    key_of = jax.random.split(jax.random.key(seed), 8)
    own_keys = jax.random.split(jax.random.fold_in(key_of[7], part), 8)
    return {
        "act": noise(own_keys[0], (TOKENS, D), 1.0, 6.0, ((0, 8), (1, 2))),
        "grad_out": noise(own_keys[1], (TOKENS, D), 1.0, 6.0, ((0, 8), (1, 2))),
        "route_ids": draw_route_ids(jax.random.fold_in(jax.random.fold_in(key_of[7], part), 71), part),
        "gate_probs": jnp.clip(jnp.exp(math.log(1.0) - 2.306499 * jax.random.uniform(own_keys[3], (TOKENS, 2), jnp.float32) ** shard_levels(own_keys[3], (TOKENS, 2), ((0, 8),), -0.2, 0.2)), 0.099609375, 1.0).astype(jnp.bfloat16),
        "w_gate": noise(key_of[4], (D, FW), D ** -0.5, 0.125, ((1, 16),)),
        "w_up": noise(key_of[5], (D, FW), D ** -0.5, 0.125, ((1, 16),)),
        "w_down": noise(key_of[6], (FW, D), FFW ** -0.5, 0.046875, ((0, 16),)),
    }


def expert_terms(rows_in, grads_in, gate_in, gate_w, up_w, down_w):
    pre_gate = jnp.dot(rows_in, gate_w, preferred_element_type=jnp.float32)
    pre_up = jnp.dot(rows_in, up_w, preferred_element_type=jnp.float32)
    hid_grad = jnp.dot(grads_in, down_w.T, preferred_element_type=jnp.float32)
    squash = jax.nn.sigmoid(pre_gate)
    active = pre_gate * squash
    hidden = active * pre_up
    gate_term = jnp.sum(hidden * hid_grad, axis=1)
    weight = gate_in.astype(jnp.float32)[:, None]
    scaled = weight * hid_grad
    grad_gate = (scaled * pre_up * squash * (1.0 + pre_gate * (1.0 - squash))).astype(jnp.bfloat16)
    grad_up = (scaled * active).astype(jnp.bfloat16)
    hidden_w = (weight * hidden).astype(jnp.bfloat16)
    down_grad = jnp.dot(hidden_w.T, grads_in, preferred_element_type=jnp.float32)
    gate_wgrad = jnp.dot(rows_in.T, grad_gate, preferred_element_type=jnp.float32)
    up_wgrad = jnp.dot(rows_in.T, grad_up, preferred_element_type=jnp.float32)
    input_grad = jnp.dot(grad_gate, gate_w.T, preferred_element_type=jnp.float32) + jnp.dot(grad_up, up_w.T, preferred_element_type=jnp.float32)
    return input_grad, gate_term, gate_wgrad, up_wgrad, down_grad


def reference(act, grad_out, route_ids, gate_probs, w_gate, w_up, w_down):
    blocks = TOKENS // TOK_DEV
    slots_all = FLIGHT * blocks * CAP
    span = blocks * CAP
    paired = route_ids.reshape(blocks, 2 * TOK_DEV).astype(jnp.int32)
    experts_ids = jnp.arange(FLIGHT).astype(jnp.int32)
    one_hot = (paired[:, :, None] == experts_ids[None, None, :]).astype(jnp.int32)
    before = jnp.cumsum(one_hot, axis=1) - one_hot
    slot_num = jnp.sum(before * one_hot, axis=2).astype(jnp.int32)
    block_num = jnp.arange(blocks).astype(jnp.int32)[:, None]
    slot_index = jnp.where(paired < FLIGHT, (paired * blocks + block_num) * CAP + slot_num, slots_all).astype(jnp.int32)
    token_num = (block_num * TOK_DEV + jnp.arange(2 * TOK_DEV).astype(jnp.int32)[None, :] // 2).astype(jnp.int32)
    flat_index = slot_index.reshape(-1)
    row_table = jnp.full((slots_all + 1,), TOKENS, jnp.int32).at[flat_index].set(token_num.reshape(-1))[:slots_all]
    gate_table = jnp.zeros((slots_all + 1,), jnp.bfloat16).at[flat_index].set(gate_probs.reshape(-1))[:slots_all]
    padded_act = jnp.concatenate([act, jnp.zeros((1, D), jnp.bfloat16)], axis=0)
    padded_grad = jnp.concatenate([grad_out, jnp.zeros((1, D), jnp.bfloat16)], axis=0)
    input_list, term_list, gate_list, up_list, down_list = [], [], [], [], []
    for expert_idx in range(FLIGHT):
        row_pick = row_table[expert_idx * span:(expert_idx + 1) * span]
        results = expert_terms(
            padded_act[row_pick], padded_grad[row_pick], gate_table[expert_idx * span:(expert_idx + 1) * span],
            w_gate[:, expert_idx * FFW:(expert_idx + 1) * FFW], w_up[:, expert_idx * FFW:(expert_idx + 1) * FFW],
            w_down[expert_idx * FFW:(expert_idx + 1) * FFW, :])
        input_list.append(results[0])
        term_list.append(results[1])
        gate_list.append(results[2])
        up_list.append(results[3])
        down_list.append(results[4])
    input_all = jnp.concatenate(input_list + [jnp.zeros((1, D), jnp.float32)], axis=0)
    term_all = jnp.concatenate(term_list + [jnp.zeros((1,), jnp.float32)], axis=0)
    d_act = jnp.sum(input_all[flat_index].reshape(TOKENS, 2, D), axis=1).astype(jnp.bfloat16)
    d_gate = term_all[flat_index].reshape(TOKENS, 2)
    dw_gate = jnp.concatenate(gate_list, axis=1).astype(jnp.bfloat16)
    dw_up = jnp.concatenate(up_list, axis=1).astype(jnp.bfloat16)
    dw_down = jnp.concatenate(down_list, axis=0).astype(jnp.bfloat16)
    return (d_act, d_gate, dw_gate, dw_up, dw_down)
```

```python
import functools

import jax
import jax.numpy as jnp
from jax import lax
from jax.experimental import pallas as pl
from jax.experimental.pallas import tpu as pltpu
from jax.sharding import PartitionSpec as P

FLIGHT = 4
CAP = 8
LANES = 128
MESH = pl.DeviceIdType.MESH
F32 = jnp.float32
BF16 = jnp.bfloat16


def dot_nt(a, b):
    return lax.dot_general(a, b, (((1,), (1,)), ((), ())), preferred_element_type=F32)


def iota(shape, dim):
    return lax.broadcasted_iota(jnp.int32, shape, dim)


def chosen(ids_ref, expert, slot):
    rows, toks = expert.shape
    id0 = jnp.broadcast_to(ids_ref[0:1, :], (rows, toks))
    id1 = jnp.broadcast_to(ids_ref[1:2, :], (rows, toks))
    first = id0 == expert
    second = id1 == expert
    member = jnp.where(first | second, 1.0, 0.0)
    earlier = jnp.where(iota((toks, toks), 0) < iota((toks, toks), 1), 1.0, 0.0)
    count = jnp.dot(member.astype(BF16), earlier.astype(BF16), preferred_element_type=F32)
    picked = jnp.where(count == slot.astype(F32), member, 0.0)
    return first, second, picked


def inner_kernel(
    ranks, group, tile, act_ref, grad_ref, ids_ref, gate_ref, wg_hbm, wu_hbm, wd_hbm,
    dact_ref, dgate_ref, rows_ref, grads_ref, gg_ref, gu_ref, hw_ref,
    wg, wu, wd, pay, rx, weight, gacc, send_a, own_a, recv_a, recv_b, acc_c, recv_c,
    wsem, s1, s2, s3, rsem, sa, ra, sb, rb, sc, rc,
):
    rank = lax.axis_index("expert")
    half = lax.axis_index("tensor")
    mine = rank // group
    member = lax.rem(rank, group)
    other = 1 - half
    toks, width = act_ref.shape
    full = width + LANES
    slots = ranks
    rows = slots * CAP
    tiles = wg.shape[0]
    dim = wg.shape[1]

    def weight_copies(j):
        col = pl.ds(pl.multiple_of(j * tile, tile), tile)
        return (
            pltpu.make_async_copy(wg_hbm.at[:, col], wg.at[j], wsem.at[0, j]),
            pltpu.make_async_copy(wu_hbm.at[:, col], wu.at[j], wsem.at[1, j]),
            pltpu.make_async_copy(wd_hbm.at[col, :], wd.at[j], wsem.at[2, j]),
        )

    @pl.loop(0, tiles)
    def _(j):
        for c in weight_copies(j):
            c.start()

    def at_plane(e):
        return {"expert": e * group + member, "tensor": half}

    def at_member(i):
        return {"expert": mine * group + i, "tensor": half}

    partner = {"expert": rank, "tensor": other}
    planes = [lax.rem(mine + d, FLIGHT) for d in range(1, FLIGHT)]
    planes_back = [lax.rem(mine + FLIGHT - d, FLIGHT) for d in range(1, FLIGHT)]
    members = [lax.rem(member + d, group) for d in range(1, group)]
    members_back = [lax.rem(member + group - d, group) for d in range(1, group)]

    barrier = pltpu.get_barrier_semaphore()
    for dev in [at_plane(e) for e in planes] + [at_member(i) for i in members] + [partner]:
        pl.semaphore_signal(barrier, inc=1, device_id=dev, device_id_type=MESH)

    r = iota((FLIGHT * 2 * CAP, toks), 0)
    expert_r = r // (2 * CAP)
    first, second, picked = chosen(ids_ref, expert_r, lax.rem(r, CAP))
    is_act = lax.rem(r // CAP, 2) == 0
    pick_a = jnp.where(is_act, picked, 0.0).astype(BF16)
    pick_g = jnp.where(is_act, 0.0, picked).astype(BF16)
    g0 = jnp.broadcast_to(gate_ref[0:1, :], r.shape)
    g1 = jnp.broadcast_to(gate_ref[1:2, :], r.shape)
    gates = jnp.sum(picked * jnp.where(first, g0, g1), axis=1, keepdims=True)
    packed = jnp.dot(pick_a, act_ref[...], preferred_element_type=F32) + jnp.dot(
        pick_g, grad_ref[...], preferred_element_type=F32
    )
    gate_block = jnp.broadcast_to(gates, (FLIGHT * 2 * CAP, LANES))
    for e in range(FLIGHT):
        at = slice(e * 2 * CAP, (e + 1) * 2 * CAP)
        pay[e, :, 0:width] = packed[at].astype(BF16)
        pay[e, :, width:full] = gate_block[at].astype(BF16)

    pl.semaphore_wait(barrier, FLIGHT - 1 + group - 1 + 1)

    here = member * FLIGHT + mine
    sends = []

    def send(src, dst, ssem, dsem, dev):
        c = pltpu.make_async_remote_copy(
            src_ref=src, dst_ref=dst, send_sem=ssem, recv_sem=dsem, device_id=dev, device_id_type=MESH
        )
        c.start()
        sends.append(c)

    def wait_slot(h, slot):
        pltpu.make_async_copy(rx.at[h, slot], rx.at[h, slot], rsem.at[h, slot]).wait()

    for d, e in enumerate(planes):
        send(pay.at[e], rx.at[half, here], s1.at[d], rsem.at[half, here], at_plane(e))
    rx[half, here] = pay[mine]

    def to_partner(slot):
        send(rx.at[half, slot], rx.at[half, slot], s3.at[slot], rsem.at[half, slot], partner)

    for z in [mine] + planes_back:
        slot = member * FLIGHT + z
        if z is not mine:
            wait_slot(half, slot)
        for d, i in enumerate(members):
            send(rx.at[half, slot], rx.at[half, slot], s2.at[d, z], rsem.at[half, slot], at_member(i))
        to_partner(slot)
    for z in [mine] + planes_back:
        for i in members_back:
            slot = i * FLIGHT + z
            wait_slot(half, slot)
            to_partner(slot)
    for slot in range(slots):
        wait_slot(other, slot)

    a = iota((rows, 2 * rows), 0)
    b = iota((rows, 2 * rows), 1)
    want = (a // CAP) * 2 * CAP + lax.rem(a, CAP)
    take_a = jnp.where(b == want, 1.0, 0.0).astype(BF16)
    take_g = jnp.where(b == want + CAP, 1.0, 0.0).astype(BF16)
    for h in range(2):
        got = rx[h].reshape(2 * rows, full)
        cols = slice(h * width, (h + 1) * width)
        rows_ref[:, cols] = jnp.dot(take_a, got[:, 0:width], preferred_element_type=F32).astype(BF16)
        grads_ref[:, cols] = jnp.dot(take_g, got[:, 0:width], preferred_element_type=F32).astype(BF16)
        if h == 0:
            weight[...] = jnp.dot(take_a, got[:, width:full], preferred_element_type=F32)
    gacc[...] = jnp.zeros_like(gacc)

    def hidden_cols(j):
        return pl.ds(pl.multiple_of(j * tile, tile), tile)

    @pl.loop(0, tiles)
    def _(j):
        for c in weight_copies(j):
            c.wait()
        pre_gate = jnp.dot(rows_ref[...], wg[j], preferred_element_type=F32)
        pre_up = jnp.dot(rows_ref[...], wu[j], preferred_element_type=F32)
        hid_grad = dot_nt(grads_ref[...], wd[j])
        sig = jax.nn.sigmoid(pre_gate)
        active = pre_gate * sig
        hidden = active * pre_up
        gacc[...] += jnp.broadcast_to(jnp.sum(hidden * hid_grad, axis=1, keepdims=True), gacc.shape)
        w = weight[:, 0:1]
        scaled = w * hid_grad
        gg_ref[:, hidden_cols(j)] = (scaled * pre_up * sig * (1.0 + pre_gate * (1.0 - sig))).astype(BF16)
        gu_ref[:, hidden_cols(j)] = (scaled * active).astype(BF16)
        hw_ref[hidden_cols(j), :] = jnp.transpose(w * hidden).astype(BF16)

    def input_terms(h, out):
        at = pl.ds(pl.multiple_of(h * width, width), width)
        out[:, width:full] = gacc[...]
        out[:, 0:width] = jnp.zeros((rows, width), F32)

        @pl.loop(0, tiles)
        def _(j):
            out[:, 0:width] += dot_nt(gg_ref[:, hidden_cols(j)], wg[j, at, :]) + dot_nt(
                gu_ref[:, hidden_cols(j)], wu[j, at, :]
            )

    input_terms(other, send_a)
    send(send_a, recv_a, sa, ra, partner)
    input_terms(half, own_a)
    pltpu.make_async_copy(recv_a, recv_a, ra).wait()
    own_a[...] += recv_a[...]

    span = FLIGHT * CAP

    def member_rows(i):
        return pl.ds(pl.multiple_of(i * span, span), span)

    for d, i in enumerate(members):
        send(own_a.at[member_rows(i)], recv_b.at[member], sb.at[d], rb.at[member], at_member(i))
    total = own_a[member_rows(member), :]
    for i in members_back:
        pltpu.make_async_copy(recv_b.at[i], recv_b.at[i], rb.at[i]).wait()
        total = total + recv_b[i]
    acc_c[...] = total

    def plane_rows(e):
        return pl.ds(pl.multiple_of(e * CAP, CAP), CAP)

    for d, e in enumerate(planes):
        send(acc_c.at[plane_rows(e)], recv_c.at[plane_rows(mine)], sc.at[d], rc.at[mine], at_plane(e))
    recv_c[plane_rows(mine), :] = acc_c[plane_rows(mine), :]

    r = iota((span, toks), 0)
    first, second, picked = chosen(ids_ref, r // CAP, lax.rem(r, CAP))
    for e in planes_back:
        part = recv_c.at[plane_rows(e)]
        pltpu.make_async_copy(part, part, rc.at[e]).wait()
    dact_ref[...] = lax.dot_general(
        picked, recv_c[:, 0:width], (((0,), (0,)), ((), ())),
        precision=lax.Precision.HIGHEST, preferred_element_type=F32,
    ).astype(BF16)
    term = picked * recv_c[:, width:width + 1]
    dgate_ref[0:1, :] = jnp.sum(jnp.where(first, term, 0.0), axis=0, keepdims=True)
    dgate_ref[1:2, :] = jnp.sum(jnp.where(second, term, 0.0), axis=0, keepdims=True)

    for c in sends:
        c.wait_send()


def weight_kernel(chunk, rows_ref, hw_ref, gg_ref, gu_ref, grads_ref, dwg_ref, dwu_ref, dwd_ref):
    rows_t = jnp.transpose(rows_ref[...].astype(F32)).astype(BF16)
    hw_t = hw_ref[...]
    for left, right, out in ((rows_t, gg_ref, dwg_ref), (rows_t, gu_ref, dwu_ref), (hw_t, grads_ref, dwd_ref)):
        cols = out.shape[1]
        step = chunk if cols % chunk == 0 else cols
        for c in range(0, cols, step):
            out[:, c:c + step] = jnp.dot(
                left, right[:, c:c + step], preferred_element_type=F32
            ).astype(BF16)


def local(act, grad_out, route_ids, gate_probs, w_gate, w_up, w_down):
    ranks = lax.axis_size("expert")
    group = ranks // FLIGHT
    toks, width = act.shape
    dim, units = w_gate.shape
    tile = 512 if units % 512 == 0 else units
    tiles = units // tile
    rows = ranks * CAP
    full = width + LANES
    span = FLIGHT * CAP
    vmem = pl.BlockSpec(memory_space=pltpu.VMEM)
    hbm = pl.BlockSpec(memory_space=pl.ANY)
    dma = pltpu.SemaphoreType.DMA
    sds = jax.ShapeDtypeStruct
    d_act, d_gate, rows_in, grads_in, grad_gate, grad_up, hidden_t = pl.pallas_call(
        functools.partial(inner_kernel, ranks, group, tile),
        out_shape=(
            sds((toks, width), BF16), sds((2, toks), F32), sds((rows, dim), BF16), sds((rows, dim), BF16),
            sds((rows, units), BF16), sds((rows, units), BF16), sds((units, rows), BF16),
        ),
        in_specs=[vmem] * 4 + [hbm] * 3,
        out_specs=(vmem,) * 7,
        scratch_shapes=[
            pltpu.VMEM((tiles, dim, tile), BF16),
            pltpu.VMEM((tiles, dim, tile), BF16),
            pltpu.VMEM((tiles, tile, dim), BF16),
            pltpu.VMEM((FLIGHT, 2 * CAP, full), BF16),
            pltpu.VMEM((2, ranks, 2 * CAP, full), BF16),
            pltpu.VMEM((rows, LANES), F32),
            pltpu.VMEM((rows, LANES), F32),
            pltpu.VMEM((rows, full), F32),
            pltpu.VMEM((rows, full), F32),
            pltpu.VMEM((rows, full), F32),
            pltpu.VMEM((group, span, full), F32),
            pltpu.VMEM((span, full), F32),
            pltpu.VMEM((span, full), F32),
            dma((3, tiles)),
            dma((FLIGHT,)),
            dma((group, FLIGHT)),
            dma((ranks,)),
            dma((2, ranks)),
            dma(()),
            dma(()),
            dma((group,)),
            dma((group,)),
            dma((FLIGHT,)),
            dma((FLIGHT,)),
        ],
        compiler_params=pltpu.CompilerParams(
            collective_id=0, has_side_effects=True, vmem_limit_bytes=60 * 1024 * 1024
        ),
        cost_estimate=pl.CostEstimate(
            flops=10 * rows * dim * units, bytes_accessed=6 * dim * units, transcendentals=rows * units
        ),
    )(act, grad_out, route_ids.T, gate_probs.astype(F32).T, w_gate, w_up, w_down)
    steps = 16
    while units % (16 * steps) or dim % (LANES * steps):
        steps //= 2
    dw_gate, dw_up, dw_down = pl.pallas_call(
        functools.partial(weight_kernel, 512),
        grid=(steps,),
        out_shape=(sds((dim, units), BF16), sds((dim, units), BF16), sds((units, dim), BF16)),
        in_specs=[
            pl.BlockSpec((rows, dim // steps), lambda g: (0, g)),
            pl.BlockSpec((units // steps, rows), lambda g: (g, 0)),
            vmem, vmem, vmem,
        ],
        out_specs=(
            pl.BlockSpec((dim // steps, units), lambda g: (g, 0)),
            pl.BlockSpec((dim // steps, units), lambda g: (g, 0)),
            pl.BlockSpec((units // steps, dim), lambda g: (g, 0)),
        ),
        compiler_params=pltpu.CompilerParams(vmem_limit_bytes=48 * 1024 * 1024),
        cost_estimate=pl.CostEstimate(
            flops=6 * rows * dim * units, bytes_accessed=6 * dim * units, transcendentals=0
        ),
    )(rows_in, hidden_t, grad_gate, grad_up, grads_in)
    return (d_act, d_gate.T, dw_gate, dw_up, dw_down)


def solution(mesh):
    return jax.shard_map(
        local,
        mesh=mesh,
        in_specs=(
            P(("dom", "expert"), "tensor"),
            P(("dom", "expert"), "tensor"),
            P(("dom", "expert"), None),
            P(("dom", "expert"), None),
            P(None, ("expert", "tensor")),
            P(None, ("expert", "tensor")),
            P(("expert", "tensor"), None),
        ),
        out_specs=(
            P(("dom", "expert"), "tensor"),
            P(("dom", "expert"), None),
            P("dom", ("expert", "tensor")),
            P("dom", ("expert", "tensor")),
            P(("expert", "tensor"), "dom"),
        ),
        check_vma=False,
    )
```

```python
import functools

import jax
import jax.numpy as jnp
from jax import lax
from jax.experimental import pallas as pl
from jax.experimental.pallas import tpu as pltpu
from jax.sharding import PartitionSpec as P

FLIGHT = 4
CAP = 8
LANES = 128
MESH = pl.DeviceIdType.MESH
F32 = jnp.float32
BF16 = jnp.bfloat16


def dot_nt(a, b):
    return lax.dot_general(a, b, (((1,), (1,)), ((), ())), preferred_element_type=F32)


def iota(shape, dim):
    return lax.broadcasted_iota(jnp.int32, shape, dim)


def chosen(ids_ref, expert, slot):
    rows, toks = expert.shape
    id0 = jnp.broadcast_to(ids_ref[0:1, :], (rows, toks))
    id1 = jnp.broadcast_to(ids_ref[1:2, :], (rows, toks))
    first = id0 == expert
    second = id1 == expert
    member = jnp.where(first | second, 1.0, 0.0)
    earlier = jnp.where(iota((toks, toks), 0) < iota((toks, toks), 1), 1.0, 0.0)
    count = jnp.dot(member.astype(BF16), earlier.astype(BF16), preferred_element_type=F32)
    picked = jnp.where(count == slot.astype(F32), member, 0.0)
    return first, second, picked


def inner_kernel(
    ranks, group, tile, act_ref, grad_ref, ids_ref, gate_ref, wg_hbm, wu_hbm, wd_hbm,
    keep_ref, give_ref, rows_ref, grads_ref, gg_ref, gu_ref, hw_ref,
    wg, wu, wd, pay, rx, weight, gacc, send_a, own_a, recv_a,
    wsem, s1, s2, s3, rsem, sa, ra,
):
    rank = lax.axis_index("expert")
    half = lax.axis_index("tensor")
    mine = rank // group
    member = lax.rem(rank, group)
    other = 1 - half
    toks, width = act_ref.shape
    full = width + LANES
    slots = ranks
    rows = slots * CAP
    tiles = wg.shape[0]
    dim = wg.shape[1]

    def weight_copies(j):
        col = pl.ds(pl.multiple_of(j * tile, tile), tile)
        return (
            pltpu.make_async_copy(wg_hbm.at[:, col], wg.at[j], wsem.at[0, j]),
            pltpu.make_async_copy(wu_hbm.at[:, col], wu.at[j], wsem.at[1, j]),
            pltpu.make_async_copy(wd_hbm.at[col, :], wd.at[j], wsem.at[2, j]),
        )

    @pl.loop(0, tiles)
    def _(j):
        for c in weight_copies(j):
            c.start()

    def at_plane(e):
        return {"expert": e * group + member, "tensor": half}

    def at_member(i):
        return {"expert": mine * group + i, "tensor": half}

    partner = {"expert": rank, "tensor": other}
    planes = [lax.rem(mine + d, FLIGHT) for d in range(1, FLIGHT)]
    planes_back = [lax.rem(mine + FLIGHT - d, FLIGHT) for d in range(1, FLIGHT)]
    members = [lax.rem(member + d, group) for d in range(1, group)]
    members_back = [lax.rem(member + group - d, group) for d in range(1, group)]

    barrier = pltpu.get_barrier_semaphore()
    for dev in [at_plane(e) for e in planes] + [at_member(i) for i in members] + [partner]:
        pl.semaphore_signal(barrier, inc=1, device_id=dev, device_id_type=MESH)

    r = iota((FLIGHT * 2 * CAP, toks), 0)
    expert_r = r // (2 * CAP)
    first, second, picked = chosen(ids_ref, expert_r, lax.rem(r, CAP))
    is_act = lax.rem(r // CAP, 2) == 0
    pick_a = jnp.where(is_act, picked, 0.0).astype(BF16)
    pick_g = jnp.where(is_act, 0.0, picked).astype(BF16)
    probs = gate_ref[...].astype(F32)
    g0 = jnp.broadcast_to(probs[0:1, :], r.shape)
    g1 = jnp.broadcast_to(probs[1:2, :], r.shape)
    gates = jnp.sum(picked * jnp.where(first, g0, g1), axis=1, keepdims=True)
    packed = jnp.dot(pick_a, act_ref[...], preferred_element_type=F32) + jnp.dot(
        pick_g, grad_ref[...], preferred_element_type=F32
    )
    gate_block = jnp.broadcast_to(gates, (FLIGHT * 2 * CAP, LANES))
    for e in range(FLIGHT):
        at = slice(e * 2 * CAP, (e + 1) * 2 * CAP)
        pay[e, :, 0:width] = packed[at].astype(BF16)
        pay[e, :, width:full] = gate_block[at].astype(BF16)

    pl.semaphore_wait(barrier, FLIGHT - 1 + group - 1 + 1)

    here = member * FLIGHT + mine
    sends = []

    def send(src, dst, ssem, dsem, dev):
        c = pltpu.make_async_remote_copy(
            src_ref=src, dst_ref=dst, send_sem=ssem, recv_sem=dsem, device_id=dev, device_id_type=MESH
        )
        c.start()
        sends.append(c)

    def wait_slot(h, slot):
        pltpu.make_async_copy(rx.at[h, slot], rx.at[h, slot], rsem.at[h, slot]).wait()

    for d, e in enumerate(planes):
        send(pay.at[e], rx.at[half, here], s1.at[d], rsem.at[half, here], at_plane(e))
    rx[half, here] = pay[mine]

    def to_partner(slot):
        send(rx.at[half, slot], rx.at[half, slot], s3.at[slot], rsem.at[half, slot], partner)

    for z in [mine] + planes_back:
        slot = member * FLIGHT + z
        if z is not mine:
            wait_slot(half, slot)
        for d, i in enumerate(members):
            send(rx.at[half, slot], rx.at[half, slot], s2.at[d, z], rsem.at[half, slot], at_member(i))
        to_partner(slot)
    for z in [mine] + planes_back:
        for i in members_back:
            slot = i * FLIGHT + z
            wait_slot(half, slot)
            to_partner(slot)
    for slot in range(slots):
        wait_slot(other, slot)

    a = iota((rows, 2 * rows), 0)
    b = iota((rows, 2 * rows), 1)
    want = (a // CAP) * 2 * CAP + lax.rem(a, CAP)
    take_a = jnp.where(b == want, 1.0, 0.0).astype(BF16)
    take_g = jnp.where(b == want + CAP, 1.0, 0.0).astype(BF16)
    for h in range(2):
        got = rx[h].reshape(2 * rows, full)
        cols = slice(h * width, (h + 1) * width)
        rows_ref[:, cols] = jnp.dot(take_a, got[:, 0:width], preferred_element_type=F32).astype(BF16)
        grads_ref[:, cols] = jnp.dot(take_g, got[:, 0:width], preferred_element_type=F32).astype(BF16)
        if h == 0:
            weight[...] = jnp.dot(take_a, got[:, width:full], preferred_element_type=F32)
    gacc[...] = jnp.zeros_like(gacc)

    def hidden_cols(j):
        return pl.ds(pl.multiple_of(j * tile, tile), tile)

    @pl.loop(0, tiles)
    def _(j):
        for c in weight_copies(j):
            c.wait()
        pre_gate = jnp.dot(rows_ref[...], wg[j], preferred_element_type=F32)
        pre_up = jnp.dot(rows_ref[...], wu[j], preferred_element_type=F32)
        hid_grad = dot_nt(grads_ref[...], wd[j])
        sig = jax.nn.sigmoid(pre_gate)
        active = pre_gate * sig
        hidden = active * pre_up
        gacc[...] += jnp.broadcast_to(jnp.sum(hidden * hid_grad, axis=1, keepdims=True), gacc.shape)
        w = weight[:, 0:1]
        scaled = w * hid_grad
        gg_ref[:, hidden_cols(j)] = (scaled * pre_up * sig * (1.0 + pre_gate * (1.0 - sig))).astype(BF16)
        gu_ref[:, hidden_cols(j)] = (scaled * active).astype(BF16)
        hw_ref[hidden_cols(j), :] = jnp.transpose(w * hidden).astype(BF16)

    def input_terms(h, out):
        at = pl.ds(pl.multiple_of(h * width, width), width)
        out[:, width:full] = gacc[...]
        out[:, 0:width] = jnp.zeros((rows, width), F32)

        @pl.loop(0, tiles)
        def _(j):
            out[:, 0:width] += dot_nt(gg_ref[:, hidden_cols(j)], wg[j, at, :]) + dot_nt(
                gu_ref[:, hidden_cols(j)], wu[j, at, :]
            )

    input_terms(other, send_a)
    send(send_a, recv_a, sa, ra, partner)
    input_terms(half, own_a)
    pltpu.make_async_copy(recv_a, recv_a, ra).wait()
    span = FLIGHT * CAP

    def both(i):
        at = pl.ds(pl.multiple_of(i * span, span), span)
        return own_a[at, :] + recv_a[at, :]

    keep_ref[...] = both(member)
    for d, i in enumerate(members):
        give_ref[d] = both(i)

    for c in sends:
        c.wait_send()


def middle_kernel(group, keep_ref, *refs):
    got, outs = refs[:-FLIGHT], refs[-FLIGHT:]
    mine = lax.axis_index("expert") // group
    for d, out in enumerate(outs):
        at = pl.ds(pl.multiple_of(lax.rem(mine + d, FLIGHT) * CAP, CAP), CAP)
        total = keep_ref[at, :]
        for g in got:
            total = total + g[at, :]
        out[...] = total


def token_kernel(group, ids_ref, *refs):
    parts, (dact_ref, dgate_ref, back) = refs[:FLIGHT], refs[FLIGHT:]
    mine = lax.axis_index("expert") // group
    width = dact_ref.shape[1]
    for d, part in enumerate(parts):
        at = pl.ds(pl.multiple_of(lax.rem(mine + FLIGHT - d, FLIGHT) * CAP, CAP), CAP)
        back[at, :] = part[...]
    r = iota((FLIGHT * CAP, dact_ref.shape[0]), 0)
    first, second, picked = chosen(ids_ref, r // CAP, lax.rem(r, CAP))
    dact_ref[...] = lax.dot_general(
        picked, back[:, 0:width], (((0,), (0,)), ((), ())),
        precision=lax.Precision.HIGHEST, preferred_element_type=F32,
    ).astype(BF16)
    term = picked * back[:, width:width + 1]
    dgate_ref[0:1, :] = jnp.sum(jnp.where(first, term, 0.0), axis=0, keepdims=True)
    dgate_ref[1:2, :] = jnp.sum(jnp.where(second, term, 0.0), axis=0, keepdims=True)


def weight_kernel(chunk, turn, left_ref, right_ref, out):
    left = left_ref[...]
    if turn:
        left = jnp.transpose(left.astype(F32)).astype(BF16)
    cols = out.shape[1]
    step = chunk if cols % chunk == 0 else cols
    for c in range(0, cols, step):
        out[:, c:c + step] = jnp.dot(left, right_ref[:, c:c + step], preferred_element_type=F32).astype(BF16)


def weight_grad(left, right, turn, steps, vmem_limit):
    depth, cols = right.shape
    count = left.shape[1] if turn else left.shape[0]
    block = count // steps
    if turn:
        left_spec = pl.BlockSpec((depth, block), lambda g: (0, g))
    else:
        left_spec = pl.BlockSpec((block, depth), lambda g: (g, 0))
    return pl.pallas_call(
        functools.partial(weight_kernel, 512, turn),
        grid=(steps,),
        out_shape=jax.ShapeDtypeStruct((count, cols), BF16),
        in_specs=[left_spec, pl.BlockSpec((depth, cols), lambda g: (0, 0))],
        out_specs=pl.BlockSpec((block, cols), lambda g: (g, 0)),
        compiler_params=pltpu.CompilerParams(vmem_limit_bytes=vmem_limit),
        cost_estimate=pl.CostEstimate(
            flops=8 * depth * count * cols, bytes_accessed=4 * count * cols, transcendentals=0
        ),
    )(left, right)


def local(act, grad_out, route_ids, gate_probs, w_gate, w_up, w_down):
    ranks = lax.axis_size("expert")
    group = ranks // FLIGHT
    toks, width = act.shape
    dim, units = w_gate.shape
    tile = 512 if units % 512 == 0 else units
    tiles = units // tile
    rows = ranks * CAP
    full = width + LANES
    span = FLIGHT * CAP
    vmem = pl.BlockSpec(memory_space=pltpu.VMEM)
    hbm = pl.BlockSpec(memory_space=pl.ANY)
    dma = pltpu.SemaphoreType.DMA
    sds = jax.ShapeDtypeStruct
    keep, give, rows_in, grads_in, grad_gate, grad_up, hidden_t = pl.pallas_call(
        functools.partial(inner_kernel, ranks, group, tile),
        out_shape=(
            sds((span, full), F32), sds((max(group - 1, 1), span, full), F32), sds((rows, dim), BF16), sds((rows, dim), BF16),
            sds((rows, units), BF16), sds((rows, units), BF16), sds((units, rows), BF16),
        ),
        in_specs=[vmem] * 4 + [hbm] * 3,
        out_specs=(vmem,) * 7,
        scratch_shapes=[
            pltpu.VMEM((tiles, dim, tile), BF16),
            pltpu.VMEM((tiles, dim, tile), BF16),
            pltpu.VMEM((tiles, tile, dim), BF16),
            pltpu.VMEM((FLIGHT, 2 * CAP, full), BF16),
            pltpu.VMEM((2, ranks, 2 * CAP, full), BF16),
            pltpu.VMEM((rows, LANES), F32),
            pltpu.VMEM((rows, LANES), F32),
            pltpu.VMEM((rows, full), F32),
            pltpu.VMEM((rows, full), F32),
            pltpu.VMEM((rows, full), F32),
            dma((3, tiles)),
            dma((FLIGHT,)),
            dma((group, FLIGHT)),
            dma((ranks,)),
            dma((2, ranks)),
            dma(()),
            dma(()),
        ],
        compiler_params=pltpu.CompilerParams(
            collective_id=0, has_side_effects=True, vmem_limit_bytes=60 * 1024 * 1024
        ),
        cost_estimate=pl.CostEstimate(
            flops=10 * rows * dim * units, bytes_accessed=6 * dim * units, transcendentals=rows * units
        ),
    )(act, grad_out, route_ids.T, gate_probs.T, w_gate, w_up, w_down)
    steps = 8
    while units % (16 * steps) or dim % (LANES * steps):
        steps //= 2
    limit = 60 * 1024 * 1024

    def member_step(d):
        return [(r, r // group * group + (r % group + d) % group) for r in range(ranks)]

    def plane_step(d):
        return [(r, ((r // group + d) % FLIGHT) * group + r % group) for r in range(ranks)]

    got = [lax.ppermute(give[d - 1], "expert", member_step(d)) for d in range(1, group)]
    dw_gate = weight_grad(rows_in, grad_gate, True, steps, limit)
    parts = pl.pallas_call(
        functools.partial(middle_kernel, group),
        out_shape=(sds((CAP, full), F32),) * FLIGHT,
        in_specs=[vmem] * (1 + len(got)),
        out_specs=(vmem,) * FLIGHT,
    )(keep, *got)
    back = [parts[0]] + [lax.ppermute(parts[d], "expert", plane_step(d)) for d in range(1, FLIGHT)]
    dw_up = weight_grad(rows_in, grad_up, True, steps, limit)
    dw_down = weight_grad(hidden_t, grads_in, False, steps, limit)
    d_act, d_gate = pl.pallas_call(
        functools.partial(token_kernel, group),
        out_shape=(sds((toks, width), BF16), sds((2, toks), F32)),
        in_specs=[vmem] * (1 + FLIGHT),
        out_specs=(vmem, vmem),
        scratch_shapes=[pltpu.VMEM((span, full), F32)],
    )(route_ids.T, *back)
    return (d_act, d_gate.T, dw_gate, dw_up, dw_down)


def solution(mesh):
    return jax.shard_map(
        local,
        mesh=mesh,
        in_specs=(
            P(("dom", "expert"), "tensor"),
            P(("dom", "expert"), "tensor"),
            P(("dom", "expert"), None),
            P(("dom", "expert"), None),
            P(None, ("expert", "tensor")),
            P(None, ("expert", "tensor")),
            P(("expert", "tensor"), None),
        ),
        out_specs=(
            P(("dom", "expert"), "tensor"),
            P(("dom", "expert"), None),
            P("dom", ("expert", "tensor")),
            P("dom", ("expert", "tensor")),
            P(("expert", "tensor"), "dom"),
        ),
        check_vma=False,
    )
```

```python
import functools

import jax
import jax.numpy as jnp
from jax import lax
from jax.experimental import pallas as pl
from jax.experimental.pallas import tpu as pltpu
from jax.sharding import PartitionSpec as P

FLIGHT = 4
CAP = 8
LANES = 128
MESH = pl.DeviceIdType.MESH
F32 = jnp.float32
BF16 = jnp.bfloat16


def dot_nt(a, b):
    return lax.dot_general(a, b, (((1,), (1,)), ((), ())), preferred_element_type=F32)


def iota(shape, dim):
    return lax.broadcasted_iota(jnp.int32, shape, dim)


def chosen(ids_ref, expert, slot):
    rows, toks = expert.shape
    id0 = jnp.broadcast_to(ids_ref[0:1, :], (rows, toks))
    id1 = jnp.broadcast_to(ids_ref[1:2, :], (rows, toks))
    first = id0 == expert
    second = id1 == expert
    member = jnp.where(first | second, 1.0, 0.0)
    earlier = jnp.where(iota((toks, toks), 0) < iota((toks, toks), 1), 1.0, 0.0)
    count = jnp.dot(member.astype(BF16), earlier.astype(BF16), preferred_element_type=F32)
    picked = jnp.where(count == slot.astype(F32), member, 0.0)
    return first, second, picked


def inner_kernel(
    ranks, group, tile, act_ref, grad_ref, ids_ref, gate_ref, wg_hbm, wu_hbm, wd_hbm,
    back_ref, rows_ref, grads_ref, gg_ref, gu_ref, hw_ref,
    wg, wu, wd, pay, rx, weight, gacc, send_a, own_a, recv_a, recv_b, acc_c, recv_c,
    wsem, s1, s2, s3, rsem, sa, ra, sb, rb, sc, rc,
):
    rank = lax.axis_index("expert")
    half = lax.axis_index("tensor")
    mine = rank // group
    member = lax.rem(rank, group)
    other = 1 - half
    toks, width = act_ref.shape
    full = width + LANES
    slots = ranks
    rows = slots * CAP
    tiles = wg.shape[0]
    dim = wg.shape[1]

    def weight_copies(j):
        col = pl.ds(pl.multiple_of(j * tile, tile), tile)
        return (
            pltpu.make_async_copy(wg_hbm.at[:, col], wg.at[j], wsem.at[0, j]),
            pltpu.make_async_copy(wu_hbm.at[:, col], wu.at[j], wsem.at[1, j]),
            pltpu.make_async_copy(wd_hbm.at[col, :], wd.at[j], wsem.at[2, j]),
        )

    @pl.loop(0, tiles)
    def _(j):
        for c in weight_copies(j):
            c.start()

    def at_plane(e):
        return {"expert": e * group + member, "tensor": half}

    def at_member(i):
        return {"expert": mine * group + i, "tensor": half}

    partner = {"expert": rank, "tensor": other}
    planes = [lax.rem(mine + d, FLIGHT) for d in range(1, FLIGHT)]
    planes_back = [lax.rem(mine + FLIGHT - d, FLIGHT) for d in range(1, FLIGHT)]
    members = [lax.rem(member + d, group) for d in range(1, group)]
    members_back = [lax.rem(member + group - d, group) for d in range(1, group)]

    barrier = pltpu.get_barrier_semaphore()
    for dev in [at_plane(e) for e in planes] + [at_member(i) for i in members] + [partner]:
        pl.semaphore_signal(barrier, inc=1, device_id=dev, device_id_type=MESH)

    r = iota((FLIGHT * 2 * CAP, toks), 0)
    expert_r = r // (2 * CAP)
    first, second, picked = chosen(ids_ref, expert_r, lax.rem(r, CAP))
    is_act = lax.rem(r // CAP, 2) == 0
    pick_a = jnp.where(is_act, picked, 0.0).astype(BF16)
    pick_g = jnp.where(is_act, 0.0, picked).astype(BF16)
    probs = gate_ref[...].astype(F32)
    g0 = jnp.broadcast_to(probs[0:1, :], r.shape)
    g1 = jnp.broadcast_to(probs[1:2, :], r.shape)
    gates = jnp.sum(picked * jnp.where(first, g0, g1), axis=1, keepdims=True)
    packed = jnp.dot(pick_a, act_ref[...], preferred_element_type=F32) + jnp.dot(
        pick_g, grad_ref[...], preferred_element_type=F32
    )
    gate_block = jnp.broadcast_to(gates, (FLIGHT * 2 * CAP, LANES))
    for e in range(FLIGHT):
        at = slice(e * 2 * CAP, (e + 1) * 2 * CAP)
        pay[e, :, 0:width] = packed[at].astype(BF16)
        pay[e, :, width:full] = gate_block[at].astype(BF16)

    pl.semaphore_wait(barrier, FLIGHT - 1 + group - 1 + 1)

    here = member * FLIGHT + mine
    sends = []

    def send(src, dst, ssem, dsem, dev):
        c = pltpu.make_async_remote_copy(
            src_ref=src, dst_ref=dst, send_sem=ssem, recv_sem=dsem, device_id=dev, device_id_type=MESH
        )
        c.start()
        sends.append(c)

    def wait_slot(h, slot):
        pltpu.make_async_copy(rx.at[h, slot], rx.at[h, slot], rsem.at[h, slot]).wait()

    for d, e in enumerate(planes):
        send(pay.at[e], rx.at[half, here], s1.at[d], rsem.at[half, here], at_plane(e))
    rx[half, here] = pay[mine]

    def to_partner(slot):
        send(rx.at[half, slot], rx.at[half, slot], s3.at[slot], rsem.at[half, slot], partner)

    for z in [mine] + planes_back:
        slot = member * FLIGHT + z
        if z is not mine:
            wait_slot(half, slot)
        for d, i in enumerate(members):
            send(rx.at[half, slot], rx.at[half, slot], s2.at[d, z], rsem.at[half, slot], at_member(i))
        to_partner(slot)
    for z in [mine] + planes_back:
        for i in members_back:
            slot = i * FLIGHT + z
            wait_slot(half, slot)
            to_partner(slot)
    for slot in range(slots):
        wait_slot(other, slot)

    a = iota((rows, 2 * rows), 0)
    b = iota((rows, 2 * rows), 1)
    want = (a // CAP) * 2 * CAP + lax.rem(a, CAP)
    take_a = jnp.where(b == want, 1.0, 0.0).astype(BF16)
    take_g = jnp.where(b == want + CAP, 1.0, 0.0).astype(BF16)
    for h in range(2):
        got = rx[h].reshape(2 * rows, full)
        cols = slice(h * width, (h + 1) * width)
        rows_ref[:, cols] = jnp.dot(take_a, got[:, 0:width], preferred_element_type=F32).astype(BF16)
        grads_ref[:, cols] = jnp.dot(take_g, got[:, 0:width], preferred_element_type=F32).astype(BF16)
        if h == 0:
            weight[...] = jnp.dot(take_a, got[:, width:full], preferred_element_type=F32)
    gacc[...] = jnp.zeros_like(gacc)

    def hidden_cols(j):
        return pl.ds(pl.multiple_of(j * tile, tile), tile)

    @pl.loop(0, tiles)
    def _(j):
        for c in weight_copies(j):
            c.wait()
        pre_gate = jnp.dot(rows_ref[...], wg[j], preferred_element_type=F32)
        pre_up = jnp.dot(rows_ref[...], wu[j], preferred_element_type=F32)
        hid_grad = dot_nt(grads_ref[...], wd[j])
        sig = jax.nn.sigmoid(pre_gate)
        active = pre_gate * sig
        hidden = active * pre_up
        gacc[...] += jnp.broadcast_to(jnp.sum(hidden * hid_grad, axis=1, keepdims=True), gacc.shape)
        w = weight[:, 0:1]
        scaled = w * hid_grad
        gg_ref[:, hidden_cols(j)] = (scaled * pre_up * sig * (1.0 + pre_gate * (1.0 - sig))).astype(BF16)
        gu_ref[:, hidden_cols(j)] = (scaled * active).astype(BF16)
        hw_ref[hidden_cols(j), :] = jnp.transpose(w * hidden).astype(BF16)

    def input_terms(h, out):
        at = pl.ds(pl.multiple_of(h * width, width), width)
        out[:, width:full] = gacc[...]
        out[:, 0:width] = jnp.zeros((rows, width), F32)

        @pl.loop(0, tiles)
        def _(j):
            out[:, 0:width] += dot_nt(gg_ref[:, hidden_cols(j)], wg[j, at, :]) + dot_nt(
                gu_ref[:, hidden_cols(j)], wu[j, at, :]
            )

    input_terms(other, send_a)
    send(send_a, recv_a, sa, ra, partner)
    input_terms(half, own_a)
    pltpu.make_async_copy(recv_a, recv_a, ra).wait()
    own_a[...] += recv_a[...]

    span = FLIGHT * CAP

    def member_rows(i):
        return pl.ds(pl.multiple_of(i * span, span), span)

    for d, i in enumerate(members):
        send(own_a.at[member_rows(i)], recv_b.at[member], sb.at[d], rb.at[member], at_member(i))
    total = own_a[member_rows(member), :]
    for i in members_back:
        pltpu.make_async_copy(recv_b.at[i], recv_b.at[i], rb.at[i]).wait()
        total = total + recv_b[i]
    acc_c[...] = total

    def plane_rows(e):
        return pl.ds(pl.multiple_of(e * CAP, CAP), CAP)

    for d, e in enumerate(planes):
        send(acc_c.at[plane_rows(e)], recv_c.at[plane_rows(mine)], sc.at[d], rc.at[mine], at_plane(e))
    recv_c[plane_rows(mine), :] = acc_c[plane_rows(mine), :]

    for e in planes_back:
        part = recv_c.at[plane_rows(e)]
        pltpu.make_async_copy(part, part, rc.at[e]).wait()
    back_ref[...] = recv_c[...]

    for c in sends:
        c.wait_send()


def weight_kernel(
    chunk, rows_ref, hw_ref, gg_ref, gu_ref, grads_ref, back_ref, ids_ref,
    dwg_hbm, dwu_hbm, dwd_hbm, dact_ref, dgate_ref, bufg, bufu, bufd, sem,
):
    steps = bufg.shape[0]

    def product(left, right_ref, buf, b):
        cols = buf.shape[2]
        step = chunk if cols % chunk == 0 else cols
        for c in range(0, cols, step):
            buf[b, :, c:c + step] = jnp.dot(
                left, right_ref[:, c:c + step], preferred_element_type=F32
            ).astype(BF16)

    def copy(buf, out, which, b):
        size = buf.shape[1]
        at = pl.ds(pl.multiple_of(b * size, size), size)
        return pltpu.make_async_copy(buf.at[b], out.at[at, :], sem.at[which, b])

    @pl.loop(0, steps)
    def _(b):
        cols, units = bufg.shape[1], bufd.shape[1]
        left = rows_ref[:, pl.ds(pl.multiple_of(b * cols, cols), cols)]
        left = jnp.transpose(left.astype(F32)).astype(BF16)
        product(left, gg_ref, bufg, b)
        copy(bufg, dwg_hbm, 0, b).start()
        product(left, gu_ref, bufu, b)
        copy(bufu, dwu_hbm, 1, b).start()
        product(hw_ref[pl.ds(pl.multiple_of(b * units, units), units), :], grads_ref, bufd, b)
        copy(bufd, dwd_hbm, 2, b).start()

    toks, width = dact_ref.shape
    r = iota((FLIGHT * CAP, toks), 0)
    first, second, picked = chosen(ids_ref, r // CAP, lax.rem(r, CAP))
    dact_ref[...] = lax.dot_general(
        picked, back_ref[:, 0:width], (((0,), (0,)), ((), ())),
        precision=lax.Precision.HIGHEST, preferred_element_type=F32,
    ).astype(BF16)
    term = picked * back_ref[:, width:width + 1]
    dgate_ref[0:1, :] = jnp.sum(jnp.where(first, term, 0.0), axis=0, keepdims=True)
    dgate_ref[1:2, :] = jnp.sum(jnp.where(second, term, 0.0), axis=0, keepdims=True)

    @pl.loop(0, steps)
    def _(b):
        copy(bufg, dwg_hbm, 0, b).wait()
        copy(bufu, dwu_hbm, 1, b).wait()
        copy(bufd, dwd_hbm, 2, b).wait()


def local(act, grad_out, route_ids, gate_probs, w_gate, w_up, w_down):
    ranks = lax.axis_size("expert")
    group = ranks // FLIGHT
    toks, width = act.shape
    dim, units = w_gate.shape
    tile = 512 if units % 512 == 0 else units
    tiles = units // tile
    rows = ranks * CAP
    full = width + LANES
    span = FLIGHT * CAP
    vmem = pl.BlockSpec(memory_space=pltpu.VMEM)
    hbm = pl.BlockSpec(memory_space=pl.ANY)
    dma = pltpu.SemaphoreType.DMA
    sds = jax.ShapeDtypeStruct
    back, rows_in, grads_in, grad_gate, grad_up, hidden_t = pl.pallas_call(
        functools.partial(inner_kernel, ranks, group, tile),
        out_shape=(
            sds((span, full), F32), sds((rows, dim), BF16), sds((rows, dim), BF16),
            sds((rows, units), BF16), sds((rows, units), BF16), sds((units, rows), BF16),
        ),
        in_specs=[vmem] * 4 + [hbm] * 3,
        out_specs=(vmem,) * 6,
        scratch_shapes=[
            pltpu.VMEM((tiles, dim, tile), BF16),
            pltpu.VMEM((tiles, dim, tile), BF16),
            pltpu.VMEM((tiles, tile, dim), BF16),
            pltpu.VMEM((FLIGHT, 2 * CAP, full), BF16),
            pltpu.VMEM((2, ranks, 2 * CAP, full), BF16),
            pltpu.VMEM((rows, LANES), F32),
            pltpu.VMEM((rows, LANES), F32),
            pltpu.VMEM((rows, full), F32),
            pltpu.VMEM((rows, full), F32),
            pltpu.VMEM((rows, full), F32),
            pltpu.VMEM((group, span, full), F32),
            pltpu.VMEM((span, full), F32),
            pltpu.VMEM((span, full), F32),
            dma((3, tiles)),
            dma((FLIGHT,)),
            dma((group, FLIGHT)),
            dma((ranks,)),
            dma((2, ranks)),
            dma(()),
            dma(()),
            dma((group,)),
            dma((group,)),
            dma((FLIGHT,)),
            dma((FLIGHT,)),
        ],
        compiler_params=pltpu.CompilerParams(
            collective_id=0, has_side_effects=True, vmem_limit_bytes=60 * 1024 * 1024
        ),
        cost_estimate=pl.CostEstimate(
            flops=10 * rows * dim * units, bytes_accessed=6 * dim * units, transcendentals=rows * units
        ),
    )(act, grad_out, route_ids.T, gate_probs.T, w_gate, w_up, w_down)
    steps = 8
    while units % (16 * steps) or dim % (LANES * steps):
        steps //= 2
    dw_gate, dw_up, dw_down, d_act, d_gate = pl.pallas_call(
        functools.partial(weight_kernel, 512),
        out_shape=(
            sds((dim, units), BF16), sds((dim, units), BF16), sds((units, dim), BF16),
            sds((toks, width), BF16), sds((2, toks), F32),
        ),
        in_specs=[vmem] * 7,
        out_specs=(hbm, hbm, hbm, vmem, vmem),
        scratch_shapes=[
            pltpu.VMEM((steps, dim // steps, units), BF16),
            pltpu.VMEM((steps, dim // steps, units), BF16),
            pltpu.VMEM((steps, units // steps, dim), BF16),
            dma((3, steps)),
        ],
        compiler_params=pltpu.CompilerParams(vmem_limit_bytes=60 * 1024 * 1024),
        cost_estimate=pl.CostEstimate(
            flops=6 * rows * dim * units, bytes_accessed=6 * dim * units, transcendentals=0
        ),
    )(rows_in, hidden_t, grad_gate, grad_up, grads_in, back, route_ids.T)
    return (d_act, d_gate.T, dw_gate, dw_up, dw_down)


def solution(mesh):
    return jax.shard_map(
        local,
        mesh=mesh,
        in_specs=(
            P(("dom", "expert"), "tensor"),
            P(("dom", "expert"), "tensor"),
            P(("dom", "expert"), None),
            P(("dom", "expert"), None),
            P(None, ("expert", "tensor")),
            P(None, ("expert", "tensor")),
            P(("expert", "tensor"), None),
        ),
        out_specs=(
            P(("dom", "expert"), "tensor"),
            P(("dom", "expert"), None),
            P("dom", ("expert", "tensor")),
            P("dom", ("expert", "tensor")),
            P(("expert", "tensor"), "dom"),
        ),
        check_vma=False,
    )
```
